512 devices in a mesh: row: 16 (over z_lo, core), col: 32 (over y, x, z_hi).
Axes of the slice: x: 4, y: 4, z: 16 (z_hi: 2, z_lo: 8; z = z_hi * 8 + z_lo), core: 2. Of those that a mesh axis runs over, the one named last changes fastest.
Arguments:
- activations: bfloat16 [1024, 5120], P('col', 'row'), may hold values from -1.5 to 1.5
- grad_output: bfloat16 [1024, 5120], P('col', 'row'), may hold values from -1.5 to 1.5
- gate_pre: bfloat16 [1024, 25600], P('row', 'col'), may hold values from -6 to 6
- up_pre: bfloat16 [1024, 25600], P('row', 'col'), may hold values from -6 to 6
- gate_weight: bfloat16 [5120, 25600], P('row', 'col'), may hold values from -0.078125 to 0.078125
- up_weight: bfloat16 [5120, 25600], P('row', 'col'), may hold values from -0.078125 to 0.078125
- down_weight: bfloat16 [25600, 5120], P('col', 'row'), may hold values from -0.0390625 to 0.0390625
Outputs:
- grad_input: float32 [1024, 5120], P('col', 'row')
- grad_gate_weight: float32 [5120, 25600], P('row', 'col')
- grad_up_weight: float32 [5120, 25600], P('row', 'col')
- grad_down_weight: float32 [25600, 5120], P('col', 'row')
The draws below stay inside these ranges and needn't reach their ends.
All inputs are finite; a program needn't handle non-finite values.
Results may differ from the reference program's by a relative error of at most 0.0029.
Values may be sent and summed in bfloat16 or wider, within the bound.
No kernel may reach another device: no remote copies, remote signals or barrier semaphores. Data moves between devices by JAX's collectives and lax.ppermute only.
A program may use at most 64 MiB of HBM per device.

```python
import jax
import jax.numpy as jnp

D = 5120
FF = 25600
TOKENS = 1024


def strengthened(result, key, source, target, shards_of, factor):
    owner, partner = [(jnp.arange(result.shape[dim]) // (result.shape[dim] // shards_of)).reshape([-1 if axis == dim else 1 for axis in range(result.ndim)]) for dim in (source, target)]
    chosen = jax.random.permutation(key, shards_of)[partner]
    strong = (owner == chosen) | (owner == (partner + shards_of // 2) % shards_of)
    return jnp.where(strong, factor * result, result)


def block_scale(key, shape, split, smallest, high):
    factor_of, own = 1.0, jax.random.fold_in(key, 6)
    for axis_at, parts in split:
        heights = jnp.exp(jax.random.uniform(jax.random.fold_in(own, axis_at), (parts,), jnp.float32, smallest / len(split), high / len(split)))
        factor_of = factor_of * jnp.repeat(heights, shape[axis_at] // parts).reshape([-1 if axis == axis_at else 1 for axis in range(len(shape))])
    return factor_of


def scatter_about(rng, dims, deviation, bound, shards=(), held_as=jnp.bfloat16):
    result = deviation * jax.random.normal(rng, dims, jnp.float32)
    if shards:
        result = result * block_scale(rng, dims, shards, -0.22, 0.18)
    return jnp.clip(result, -bound, bound).astype(held_as)


def noise_with(stream_key, shape, deviation, bound, pieces, heavy, dtype=jnp.bfloat16):
    array = deviation * jax.random.normal(stream_key, shape, jnp.float32)
    if pieces:
        array = array * block_scale(stream_key, shape, pieces, -0.22, 0.18)
    return jnp.clip(strengthened(array, jax.random.fold_in(stream_key, 3), *heavy), -bound, bound).astype(dtype)


def setup_inputs(seed: int = 0) -> dict:
    key_list = jax.random.split(jax.random.key(seed), 8)
    activations = scatter_about(key_list[0], (TOKENS, D), 0.25, 1.5, ((0, 32), (1, 16)))
    grad_output = noise_with(key_list[1], (TOKENS, D), 0.25, 1.5, ((0, 32), (1, 16)), (1, 0, 32, 2.75))
    gate_pre = scatter_about(key_list[2], (TOKENS, FF), 1.0, 6.0, ((0, 16), (1, 32)))
    up_pre = scatter_about(key_list[3], (TOKENS, FF), 1.0, 6.0, ((0, 16), (1, 32)))
    gate_weight = scatter_about(key_list[4], (D, FF), D ** -0.5, 0.078125, ((0, 16), (1, 32)))
    up_weight = scatter_about(key_list[5], (D, FF), D ** -0.5, 0.078125, ((0, 16), (1, 32)))
    down_weight = scatter_about(key_list[6], (FF, D), FF ** -0.5, 0.0390625, ((0, 32), (1, 16)))
    return dict(activations=activations, grad_output=grad_output, gate_pre=gate_pre, up_pre=up_pre, gate_weight=gate_weight, up_weight=up_weight, down_weight=down_weight)


def swiglu_back(gate_vals, up_vals, grad_hidden):
    gate_wide = gate_vals.astype(jnp.float32)
    up_wide = up_vals.astype(jnp.float32)
    logistic = jax.nn.sigmoid(gate_wide)
    silu_val = gate_wide * logistic
    hidden = (silu_val * up_wide).astype(jnp.bfloat16)
    grad_gate = (grad_hidden * up_wide * logistic * (1.0 + gate_wide * (1.0 - logistic))).astype(jnp.bfloat16)
    grad_up = (grad_hidden * silu_val).astype(jnp.bfloat16)
    return hidden, grad_gate, grad_up


def reference(activations, grad_output, gate_pre, up_pre, gate_weight, up_weight, down_weight):
    grad_hidden = jnp.dot(grad_output, down_weight.T, preferred_element_type=jnp.float32)
    hidden, grad_gate, grad_up = swiglu_back(gate_pre, up_pre, grad_hidden)
    grad_down_weight = jnp.dot(hidden.T, grad_output, preferred_element_type=jnp.float32)
    grad_gate_weight = jnp.dot(activations.T, grad_gate, preferred_element_type=jnp.float32)
    grad_up_weight = jnp.dot(activations.T, grad_up, preferred_element_type=jnp.float32)
    grad_input = jnp.dot(grad_gate, gate_weight.T, preferred_element_type=jnp.float32) + jnp.dot(grad_up, up_weight.T, preferred_element_type=jnp.float32)
    return (grad_input, grad_gate_weight, grad_up_weight, grad_down_weight)
```

```python
import jax
import jax.numpy as jnp
from jax import lax
from jax.sharding import Mesh
from jax.sharding import PartitionSpec as P

F32, F16, BF16 = jnp.float32, jnp.float16, jnp.bfloat16

SIZES = dict(p=2, q=2, r=2, c=2, y=4, v=2, w=2, h=2)
ROW, COL = ("p", "q", "r", "c"), ("y", "v", "w", "h")
LINE, QUAD, PLANE = ("p", "q", "r"), ("q", "r"), ("w", "y", "v")


def swap(x, axis):
    return lax.ppermute(x, axis, [(0, 1), (1, 0)])


def halves(x, at):
    n = x.shape[0] // 2
    return (
        lax.dynamic_slice_in_dim(x, at * n, n, 0),
        lax.dynamic_slice_in_dim(x, (1 - at) * n, n, 0),
    )


def right_trans(left, right):
    return lax.dot_general(left, right, (((1,), (1,)), ((), ())), preferred_element_type=F32)


def left_trans(left, right):
    return lax.dot_general(left, right, (((0,), (0,)), ((), ())), preferred_element_type=F32)


def encode(x, bound):
    power = jnp.clip(14.0 - jnp.ceil(jnp.log2(bound)), -100.0, 100.0)
    tail = jnp.full(x.shape[:-1] + (1,), power, F32)
    return jnp.concatenate([x * jnp.exp2(power), tail], axis=-1).astype(F16)


def decode(coded):
    wide = coded.astype(F32)
    return wide[..., :-1] * jnp.exp2(-wide[..., -1:])


def bound_of(coded):
    return jnp.exp2(15.0 - coded[..., 0, -1].astype(F32))


def plane_gather(x):
    got = lax.all_to_all(jnp.broadcast_to(x[None], (16,) + x.shape), PLANE, 0, 0, tiled=True)
    return got.reshape((16 * x.shape[0],) + x.shape[1:])


def shards(activations, grad_output, gate_pre, up_pre, gate_weight, up_weight, down_weight):
    core, run = lax.axis_index("c"), lax.axis_index("h")

    saved = lax.all_gather(jnp.stack([gate_pre, up_pre]), LINE, axis=1, tiled=True)
    saved_other = swap(saved, "c")

    pair = lax.all_gather(jnp.stack([grad_output, activations]), "h", axis=1, tiled=True)
    grad_rows = plane_gather(pair[0])
    act_rows = plane_gather(pair[1])
    down_other = swap(down_weight, "c")

    mine, theirs = halves(grad_rows, core)
    given = swap(theirs, "c")
    part = right_trans(mine, down_weight) + right_trans(given, down_other)
    top = jnp.maximum(jnp.max(jnp.abs(grad_rows)), jnp.max(jnp.abs(given))).astype(F32)
    heavy = jnp.maximum(jnp.max(jnp.abs(down_weight)), jnp.max(jnp.abs(down_other))).astype(F32)
    bound = 2.0 * down_weight.shape[1] * top * heavy

    coded = encode(part, bound).reshape(4, 128, -1)
    coded = lax.all_to_all(coded, QUAD, 0, 0, tiled=True)
    part = jnp.sum(decode(coded), axis=0)
    bound = jnp.sum(bound_of(coded))
    coded = encode(part, bound)
    far = swap(coded, "p")
    part = decode(coded) + decode(far)
    bound = bound_of(coded) + bound_of(far)
    coded = lax.all_gather(encode(part, bound), QUAD, axis=0, tiled=True)
    coded_other = swap(coded, "c")

    def by_core(own, other):
        first = jnp.where(core == 0, own, other)
        second = jnp.where(core == 0, other, own)
        return jnp.concatenate([first, second], axis=0)

    gate_wide = by_core(saved[0], saved_other[0]).astype(F32)
    up_wide = by_core(saved[1], saved_other[1]).astype(F32)
    logistic = jax.nn.sigmoid(gate_wide)
    silu_val = gate_wide * logistic
    hidden = (silu_val * up_wide).astype(BF16)
    gate_slope = up_wide * logistic * (1.0 + gate_wide * (1.0 - logistic))

    grad_down_weight = left_trans(hidden, grad_rows)

    grad_hidden = by_core(decode(coded), decode(coded_other))
    grad_gate = (grad_hidden * gate_slope).astype(BF16)
    grad_up = (grad_hidden * silu_val).astype(BF16)

    share = right_trans(grad_gate, gate_weight) + right_trans(grad_up, up_weight)
    share = lax.all_to_all(share.astype(BF16).reshape(16, 64, -1), PLANE, 0, 0, tiled=True)
    share = jnp.sum(share.astype(F32), axis=0)
    near, away = halves(share, run)
    grad_input = near + swap(away, "h")

    grad_gate_weight = left_trans(act_rows, grad_gate)
    grad_up_weight = left_trans(act_rows, grad_up)
    return (grad_input, grad_gate_weight, grad_up_weight, grad_down_weight)


def solution(mesh):
    fine = Mesh(mesh.devices.reshape(tuple(SIZES.values())), tuple(SIZES))
    wide, units, down = P(COL, ROW), P(ROW, COL), P(COL, ROW)
    return jax.shard_map(
        shards,
        mesh=fine,
        in_specs=(wide, wide, units, units, units, units, down),
        out_specs=(wide, units, units, down),
        check_vma=False,
    )
```

```python
import jax
import jax.numpy as jnp
from jax import lax
from jax.sharding import Mesh
from jax.sharding import PartitionSpec as P

F32, F16, BF16 = jnp.float32, jnp.float16, jnp.bfloat16

SIZES = dict(p=2, q=2, r=2, c=2, y=4, v=2, w=2, h=2)
ROW, COL = ("p", "q", "r", "c"), ("y", "v", "w", "h")
LINE, QUAD, PLANE = ("p", "q", "r"), ("q", "r"), ("w", "y", "v")
UNITS = 200
TAIL = 8


def swap(x, axis):
    return lax.ppermute(x, axis, [(0, 1), (1, 0)])


def halves(x, at):
    n = x.shape[0] // 2
    return (
        lax.dynamic_slice_in_dim(x, at * n, n, 0),
        lax.dynamic_slice_in_dim(x, (1 - at) * n, n, 0),
    )


def dot(left, right, of_left, of_right):
    return lax.dot_general(
        left, right, (((of_left,), (of_right,)), ((), ())), preferred_element_type=F32
    )


def encode(x, power):
    tail = jnp.broadcast_to(power, x.shape[:-2] + (TAIL, x.shape[-1]))
    return jnp.concatenate([x * jnp.exp2(power), tail], axis=-2).astype(F16)


def decode(coded):
    wide = coded.astype(F32)
    power = wide[..., UNITS : UNITS + 1, :]
    return wide[..., :UNITS, :] * jnp.exp2(-power), power


def plane_gather(x):
    got = lax.all_to_all(jnp.broadcast_to(x[None], (16,) + x.shape), PLANE, 0, 0, tiled=True)
    return got.reshape((16 * x.shape[0],) + x.shape[1:])


def largest(*arrays):
    return jnp.max(jnp.stack([jnp.max(jnp.abs(a)) for a in arrays])).astype(F32)


def opening(grad_output, activations, down_weight):
    core, run = lax.axis_index("c"), lax.axis_index("h")
    near = jnp.stack([grad_output, activations])
    away = swap(near, "h")
    pair = jnp.concatenate(
        [jnp.where(run == 0, near, away), jnp.where(run == 0, away, near)], axis=1
    )
    grad_rows = plane_gather(pair[0])
    down_other = swap(down_weight, "c")

    mine, theirs = halves(grad_rows, core)
    given = swap(theirs, "c")
    part = dot(down_weight, mine, 1, 1) + dot(down_other, given, 1, 1)
    bound = 640.0 * largest(grad_rows, given) * largest(down_weight, down_other)
    power = jnp.clip(13.0 - jnp.ceil(jnp.log2(bound)), -100.0, 100.0)
    coded = encode(part.reshape(4, UNITS, 512), jnp.full((1, 1, 512), power))
    return coded, grad_rows, pair[1]


def shards(activations, grad_output, gate_pre, up_pre, gate_weight, up_weight, down_weight):
    core, run = lax.axis_index("c"), lax.axis_index("h")

    saved = lax.all_gather(jnp.stack([gate_pre, up_pre]), LINE, axis=1, tiled=True)
    coded, grad_rows, act_pair = lax.cond(
        run < 2,
        opening,
        lambda *_: (
            jnp.zeros((4, UNITS + TAIL, 512), F16),
            jnp.zeros((1024, 320), BF16),
            jnp.zeros((64, 320), BF16),
        ),
        grad_output,
        activations,
        down_weight,
    )

    saved_other = swap(saved, "c")
    parts, powers = decode(lax.all_to_all(coded, QUAD, 0, 0, tiled=True))
    coded = encode(jnp.sum(parts, axis=0), jnp.min(powers, axis=0) - 2.0)
    coded, act_pair = lax.optimization_barrier((coded, act_pair))
    far = swap(coded, "p")
    act_rows = plane_gather(act_pair)

    def by_core(own, other):
        first = jnp.where(core == 0, own, other)
        second = jnp.where(core == 0, other, own)
        return jnp.concatenate([first, second], axis=1)

    gate_wide = by_core(saved[0].T, saved_other[0].T).astype(F32)
    up_wide = by_core(saved[1].T, saved_other[1].T).astype(F32)
    logistic = jax.nn.sigmoid(gate_wide)
    silu_val = gate_wide * logistic
    hidden = (silu_val * up_wide).astype(BF16)
    gate_slope = up_wide * logistic * (1.0 + gate_wide * (1.0 - logistic))

    part, power = decode(coded)
    far_part, far_power = decode(far)
    coded = encode(part + far_part, jnp.minimum(power, far_power) - 1.0)
    coded, act_rows, silu_val, gate_slope, hidden = lax.optimization_barrier(
        (coded, act_rows, silu_val, gate_slope, hidden)
    )
    coded = lax.all_gather(coded, QUAD, axis=0, tiled=False)
    coded_other = swap(coded, "c")

    grad_down_weight = dot(hidden, grad_rows, 1, 0)

    own, other = decode(coded)[0].reshape(800, 512), decode(coded_other)[0].reshape(800, 512)
    grad_hidden = by_core(own, other)
    grad_gate = (grad_hidden * gate_slope).astype(BF16)
    grad_up = (grad_hidden * silu_val).astype(BF16)

    share = dot(grad_gate, gate_weight, 0, 1) + dot(grad_up, up_weight, 0, 1)
    share = lax.all_to_all(share.astype(BF16).reshape(16, 64, 320), PLANE, 0, 0, tiled=True)
    share = jnp.sum(share.astype(F32), axis=0)
    near, away = halves(share, run)
    grad_input = near + swap(away, "h")

    grad_gate_weight = dot(act_rows, grad_gate, 0, 1)
    grad_up_weight = dot(act_rows, grad_up, 0, 1)
    return (grad_input, grad_gate_weight, grad_up_weight, grad_down_weight)


def solution(mesh):
    fine = Mesh(mesh.devices.reshape(tuple(SIZES.values())), tuple(SIZES))
    wide, units, down = P(COL, ROW), P(ROW, COL), P(COL, ROW)
    return jax.shard_map(
        shards,
        mesh=fine,
        in_specs=(wide, wide, units, units, units, units, down),
        out_specs=(wide, units, units, down),
        check_vma=False,
    )
```

```python
import jax
import jax.numpy as jnp
from jax import lax
from jax.experimental.layout import Layout, with_layout_constraint
from jax.sharding import Mesh
from jax.sharding import PartitionSpec as P

F32, F16, BF16 = jnp.float32, jnp.float16, jnp.bfloat16

SIZES = dict(p=2, q=2, r=2, c=2, y=4, v=2, w=2, h=2)
ROW, COL = ("p", "q", "r", "c"), ("y", "v", "w", "h")
LINE, QUAD, PLANE = ("p", "q", "r"), ("q", "r"), ("w", "y", "v")
UNITS = 200
TAIL = 8


def swap(x, axis):
    return lax.ppermute(x, axis, [(0, 1), (1, 0)])


def halves(x, at):
    n = x.shape[0] // 2
    return (
        lax.dynamic_slice_in_dim(x, at * n, n, 0),
        lax.dynamic_slice_in_dim(x, (1 - at) * n, n, 0),
    )


def dot(left, right, of_left, of_right):
    return lax.dot_general(
        left, right, (((of_left,), (of_right,)), ((), ())), preferred_element_type=F32
    )


def encode(x, power):
    tail = jnp.broadcast_to(power, x.shape[:-2] + (TAIL, x.shape[-1]))
    return jnp.concatenate([x * jnp.exp2(power), tail], axis=-2).astype(F16)


def decode(coded):
    wide = coded.astype(F32)
    power = wide[..., UNITS : UNITS + 1, :]
    return wide[..., :UNITS, :] * jnp.exp2(-power), power


def plane_gather(x):
    got = lax.all_to_all(jnp.broadcast_to(x[None], (16,) + x.shape), PLANE, 0, 0, tiled=True)
    return got.reshape((16 * x.shape[0],) + x.shape[1:])


def largest(*arrays):
    return jnp.max(jnp.stack([jnp.max(jnp.abs(a)) for a in arrays])).astype(F32)


def opening(grad_output, activations, down_weight):
    core, run = lax.axis_index("c"), lax.axis_index("h")
    near = jnp.stack([grad_output, activations])
    away = swap(near, "h")
    pair = jnp.concatenate(
        [jnp.where(run == 0, near, away), jnp.where(run == 0, away, near)], axis=1
    )
    grad_rows = plane_gather(pair[0])
    down_other = swap(down_weight, "c")

    mine, theirs = halves(grad_rows, core)
    given = swap(theirs, "c")
    part = dot(down_weight, mine, 1, 1) + dot(down_other, given, 1, 1)
    bound = 640.0 * largest(grad_rows, given) * largest(down_weight, down_other)
    power = jnp.clip(13.0 - jnp.ceil(jnp.log2(bound)), -100.0, 100.0)
    coded = encode(part.reshape(4, UNITS, 512), jnp.full((1, 1, 512), power))
    return coded, grad_rows, pair[1]


def shards(activations, grad_output, gate_pre, up_pre, gate_weight, up_weight, down_weight):
    core, run = lax.axis_index("c"), lax.axis_index("h")

    saved = jnp.pad(jnp.concatenate([gate_pre, up_pre]), ((0, 0), (0, 96)))
    saved = lax.all_gather(saved, LINE, axis=0, tiled=False)
    coded, grad_rows, act_pair = lax.cond(
        run < 2,
        opening,
        lambda *_: (
            jnp.zeros((4, UNITS + TAIL, 512), F16),
            jnp.zeros((1024, 320), BF16),
            jnp.zeros((64, 320), BF16),
        ),
        grad_output,
        activations,
        down_weight,
    )

    saved_other = swap(saved, "c")
    parts, powers = decode(lax.all_to_all(coded, QUAD, 0, 0, tiled=True))
    coded = encode(jnp.sum(parts, axis=0), jnp.min(powers, axis=0) - 2.0)
    coded, act_pair = lax.optimization_barrier((coded, act_pair))
    far = swap(coded, "p")
    act_rows = plane_gather(act_pair)

    def by_core(own, other):
        first = jnp.where(core == 0, own, other)
        second = jnp.where(core == 0, other, own)
        return jnp.concatenate([first, second], axis=1)

    def turned(rows):
        rows = rows[..., :800].reshape(512, 800).T
        return with_layout_constraint(rows, Layout(major_to_minor=(0, 1)))

    def projection(rows):
        return by_core(turned(saved[:, rows]), turned(saved_other[:, rows])).astype(F32)

    gate_wide, up_wide = projection(slice(0, 64)), projection(slice(64, 128))
    logistic = jax.nn.sigmoid(gate_wide)
    silu_val = gate_wide * logistic
    hidden = (silu_val * up_wide).astype(BF16)
    gate_slope = up_wide * logistic * (1.0 + gate_wide * (1.0 - logistic))

    far, act_rows, silu_val, gate_slope, hidden = lax.optimization_barrier(
        (far, act_rows, silu_val, gate_slope, hidden)
    )
    part, power = decode(coded)
    far_part, far_power = decode(far)
    coded = encode(part + far_part, jnp.minimum(power, far_power) - 1.0)
    coded = lax.all_gather(coded, QUAD, axis=0, tiled=False)
    coded_other = swap(coded, "c")

    grad_down_weight = dot(hidden, grad_rows, 1, 0)

    own, other = decode(coded)[0].reshape(800, 512), decode(coded_other)[0].reshape(800, 512)
    grad_hidden = by_core(own, other)
    grad_gate = (grad_hidden * gate_slope).astype(BF16)
    grad_up = (grad_hidden * silu_val).astype(BF16)

    share = dot(grad_gate, gate_weight, 0, 1) + dot(grad_up, up_weight, 0, 1)
    share = with_layout_constraint(share.astype(BF16), Layout(major_to_minor=(0, 1)))
    share = lax.all_to_all(share.reshape(16, 64, 320), PLANE, 0, 0, tiled=True)
    share = jnp.sum(share.astype(F32), axis=0)
    near, away = halves(share, run)
    grad_input = near + swap(away, "h")

    grad_gate_weight = dot(act_rows, grad_gate, 0, 1)
    grad_up_weight = dot(act_rows, grad_up, 0, 1)
    return (grad_input, grad_gate_weight, grad_up_weight, grad_down_weight)


def solution(mesh):
    fine = Mesh(mesh.devices.reshape(tuple(SIZES.values())), tuple(SIZES))
    wide, units, down = P(COL, ROW), P(ROW, COL), P(COL, ROW)
    return jax.shard_map(
        shards,
        mesh=fine,
        in_specs=(wide, wide, units, units, units, units, down),
        out_specs=(wide, units, units, down),
        check_vma=False,
    )
```

```python
import jax
import jax.numpy as jnp
from jax import lax
from jax.experimental.layout import Layout, with_layout_constraint
from jax.sharding import Mesh
from jax.sharding import PartitionSpec as P

F32, F16, BF16 = jnp.float32, jnp.float16, jnp.bfloat16

SIZES = dict(p=2, q=2, r=2, c=2, y=4, v=2, w=2, h=2)
ROW, COL = ("p", "q", "r", "c"), ("y", "v", "w", "h")
LINE, QUAD, PLANE = ("p", "q", "r"), ("q", "r"), ("w", "y", "v")
UNITS = 200
TAIL = 8


def swap(x, axis):
    return lax.ppermute(x, axis, [(0, 1), (1, 0)])


def halves(x, at):
    n = x.shape[0] // 2
    return (
        lax.dynamic_slice_in_dim(x, at * n, n, 0),
        lax.dynamic_slice_in_dim(x, (1 - at) * n, n, 0),
    )


def dot(left, right, of_left, of_right):
    return lax.dot_general(
        left, right, (((of_left,), (of_right,)), ((), ())), preferred_element_type=F32
    )


def encode(x, power):
    tail = jnp.broadcast_to(power, x.shape[:-2] + (TAIL, x.shape[-1]))
    return jnp.concatenate([x * jnp.exp2(power), tail], axis=-2).astype(F16)


def decode(coded):
    wide = coded.astype(F32)
    power = wide[..., UNITS : UNITS + 1, :]
    return wide[..., :UNITS, :] * jnp.exp2(-power), power


def plane_gather(x):
    got = lax.all_to_all(jnp.broadcast_to(x[None], (16,) + x.shape), PLANE, 0, 0, tiled=True)
    return got.reshape((16 * x.shape[0],) + x.shape[1:])


def largest(*arrays):
    return jnp.max(jnp.stack([jnp.max(jnp.abs(a)) for a in arrays])).astype(F32)


def opening(grad_output, activations, down_weight):
    core = lax.axis_index("c")
    near = jnp.stack([grad_output, activations])
    pair = jnp.concatenate([near, swap(near, "h")], axis=1)
    grad_rows = plane_gather(pair[0])
    down_weight = jnp.pad(down_weight.reshape(4, UNITS, 320), ((0, 0), (0, TAIL), (0, 0)))
    down_weight = down_weight.reshape(4 * (UNITS + TAIL), 320)
    down_other = swap(down_weight, "c")

    mine, theirs = halves(grad_rows, core)
    given = swap(theirs, "c")
    part = dot(down_weight, mine, 1, 1) + dot(down_other, given, 1, 1)
    bound = 640.0 * largest(grad_rows, given) * largest(down_weight, down_other)
    power = jnp.clip(13.0 - jnp.ceil(jnp.log2(bound)), -100.0, 100.0)
    part = part.reshape(4, UNITS + TAIL, 512)
    tail = lax.broadcasted_iota(jnp.int32, part.shape, 1) >= UNITS
    coded = jnp.where(tail, power, part * jnp.exp2(power)).astype(F16)
    return coded, grad_rows, pair[1]


def shards(activations, grad_output, gate_pre, up_pre, gate_weight, up_weight, down_weight):
    core, run = lax.axis_index("c"), lax.axis_index("h")

    saved = jnp.stack([gate_pre, up_pre]).reshape(2, 2, 32, 800)
    saved = jnp.where(run == 0, saved, saved[:, ::-1]).reshape(128, 800)
    saved = jnp.pad(saved, ((0, 0), (0, 96)))
    saved = lax.all_gather(saved, LINE, axis=0, tiled=False)
    coded, grad_rows, act_pair = lax.cond(
        run < 2,
        opening,
        lambda *_: (
            jnp.zeros((4, UNITS + TAIL, 512), F16),
            jnp.zeros((1024, 320), BF16),
            jnp.zeros((64, 320), BF16),
        ),
        grad_output,
        activations,
        down_weight,
    )

    saved_other = swap(saved, "c")
    parts, powers = decode(lax.all_to_all(coded, QUAD, 0, 0, tiled=True))
    coded = encode(jnp.sum(parts, axis=0), jnp.min(powers, axis=0) - 2.0)
    coded, act_pair = lax.optimization_barrier((coded, act_pair))
    far = swap(coded, "p")
    act_rows = plane_gather(act_pair)

    def by_core(own, other):
        first = jnp.where(core == 0, own, other)
        second = jnp.where(core == 0, other, own)
        return jnp.concatenate([first, second], axis=1)

    def turned(rows):
        rows = rows[..., :800].reshape(512, 800).T
        return with_layout_constraint(rows, Layout(major_to_minor=(0, 1)))

    def projection(rows):
        return by_core(turned(saved[:, rows]), turned(saved_other[:, rows])).astype(F32)

    gate_wide, up_wide = projection(slice(0, 64)), projection(slice(64, 128))
    logistic = jax.nn.sigmoid(gate_wide)
    silu_val = gate_wide * logistic
    hidden = (silu_val * up_wide).astype(BF16)
    gate_slope = up_wide * logistic * (1.0 + gate_wide * (1.0 - logistic))

    far, act_rows, silu_val, gate_slope, hidden = lax.optimization_barrier(
        (far, act_rows, silu_val, gate_slope, hidden)
    )
    part, power = decode(coded)
    far_part, far_power = decode(far)
    coded = encode(part + far_part, jnp.minimum(power, far_power) - 1.0)
    coded = lax.all_gather(coded, QUAD, axis=0, tiled=False)
    coded_other = swap(coded, "c")

    grad_down_weight = dot(hidden, grad_rows, 1, 0)

    own, other = decode(coded)[0].reshape(800, 512), decode(coded_other)[0].reshape(800, 512)
    grad_hidden = by_core(own, other)
    grad_gate = (grad_hidden * gate_slope).astype(BF16)
    grad_up = (grad_hidden * silu_val).astype(BF16)

    share = dot(grad_gate, gate_weight, 0, 1) + dot(grad_up, up_weight, 0, 1)
    share = with_layout_constraint(share.astype(BF16), Layout(major_to_minor=(0, 1)))
    share = lax.all_to_all(share.reshape(16, 64, 320), PLANE, 0, 0, tiled=True)
    share = jnp.sum(share.astype(F32), axis=0)
    grad_input = share[:32] + swap(share[32:], "h")

    grad_gate_weight = dot(act_rows, grad_gate, 0, 1)
    grad_up_weight = dot(act_rows, grad_up, 0, 1)
    return (grad_input, grad_gate_weight, grad_up_weight, grad_down_weight)


def solution(mesh):
    fine = Mesh(mesh.devices.reshape(tuple(SIZES.values())), tuple(SIZES))
    wide, units, down = P(COL, ROW), P(ROW, COL), P(COL, ROW)
    return jax.shard_map(
        shards,
        mesh=fine,
        in_specs=(wide, wide, units, units, units, units, down),
        out_specs=(wide, units, units, down),
        check_vma=False,
    )
```

```python
import jax
import jax.numpy as jnp
from jax import lax
from jax.experimental.layout import Layout, with_layout_constraint
from jax.sharding import Mesh
from jax.sharding import PartitionSpec as P

F32, F16, BF16 = jnp.float32, jnp.float16, jnp.bfloat16

SIZES = dict(p=2, q=2, r=2, c=2, y=4, v=2, w=2, h=2)
ROW, COL = ("p", "q", "r", "c"), ("y", "v", "w", "h")
LINE, QUAD, PLANE = ("p", "q", "r"), ("q", "r"), ("w", "y", "v")
UNITS = 200
TAIL = 8


def swap(x, axis):
    return lax.ppermute(x, axis, [(0, 1), (1, 0)])


def halves(x, at):
    n = x.shape[0] // 2
    return (
        lax.dynamic_slice_in_dim(x, at * n, n, 0),
        lax.dynamic_slice_in_dim(x, (1 - at) * n, n, 0),
    )


def dot(left, right, of_left, of_right):
    return lax.dot_general(
        left, right, (((of_left,), (of_right,)), ((), ())), preferred_element_type=F32
    )


def encode(x, power):
    tail = jnp.broadcast_to(power, x.shape[:-2] + (TAIL, x.shape[-1]))
    return jnp.concatenate([x * jnp.exp2(power), tail], axis=-2).astype(F16)


def decode(coded):
    wide = coded.astype(F32)
    power = wide[..., UNITS : UNITS + 1, :]
    return wide[..., :UNITS, :] * jnp.exp2(-power), power


def plane_gather(x):
    got = lax.all_to_all(jnp.broadcast_to(x[None], (16,) + x.shape), PLANE, 0, 0, tiled=True)
    return got.reshape((16 * x.shape[0],) + x.shape[1:])


def largest(*arrays):
    return jnp.max(jnp.stack([jnp.max(jnp.abs(a)) for a in arrays])).astype(F32)


def opening(grad_output, activations, down_weight):
    core = lax.axis_index("c")
    near = jnp.stack([grad_output, activations])
    pair = jnp.concatenate([near, swap(near, "h")], axis=1)
    grad_rows = plane_gather(pair[0])
    down_weight = jnp.pad(down_weight.reshape(4, UNITS, 320), ((0, 0), (0, TAIL), (0, 0)))
    down_weight = down_weight.reshape(4 * (UNITS + TAIL), 320)
    down_other = swap(down_weight, "c")

    mine, theirs = halves(grad_rows, core)
    given = swap(theirs, "c")
    part = dot(down_weight, mine, 1, 1) + dot(down_other, given, 1, 1)
    bound = 640.0 * largest(grad_rows, given) * largest(down_weight, down_other)
    power = jnp.clip(13.0 - jnp.ceil(jnp.log2(bound)), -100.0, 100.0)
    part = part.reshape(4, UNITS + TAIL, 512)
    tail = lax.broadcasted_iota(jnp.int32, part.shape, 1) >= UNITS
    coded = jnp.where(tail, power, part * jnp.exp2(power)).astype(F16)
    return coded, grad_rows, pair[1]


def shards(activations, grad_output, gate_pre, up_pre, gate_weight, up_weight, down_weight):
    core, run = lax.axis_index("c"), lax.axis_index("h")

    saved = jnp.stack([gate_pre, up_pre]).reshape(2, 2, 32, 800)
    saved = jnp.where(run == 0, saved, saved[:, ::-1]).reshape(128, 800)
    saved = jnp.pad(saved, ((0, 0), (0, 96)))
    saved = lax.all_gather(saved, LINE, axis=0, tiled=False)
    coded, grad_rows, act_pair = lax.cond(
        run < 2,
        opening,
        lambda *_: (
            jnp.zeros((4, UNITS + TAIL, 512), F16),
            jnp.zeros((1024, 320), BF16),
            jnp.zeros((64, 320), BF16),
        ),
        grad_output,
        activations,
        down_weight,
    )

    saved_other = swap(saved, "c")
    parts, powers = decode(lax.all_to_all(coded, QUAD, 0, 0, tiled=True))
    coded = encode(jnp.sum(parts, axis=0), jnp.min(powers, axis=0) - 2.0)
    coded, act_pair = lax.optimization_barrier((coded, act_pair))
    far = swap(coded, "p")
    act_rows = plane_gather(act_pair)

    def by_core(own, other):
        first = jnp.where(core == 0, own, other)
        second = jnp.where(core == 0, other, own)
        return jnp.concatenate([first, second], axis=1)

    def turned(rows):
        rows = rows[..., :800].reshape(512, 800).T
        return with_layout_constraint(rows, Layout(major_to_minor=(0, 1)))

    def projection(rows):
        return by_core(turned(saved[:, rows]), turned(saved_other[:, rows])).astype(F32)

    gate_wide, up_wide = projection(slice(0, 64)), projection(slice(64, 128))
    logistic = jax.nn.sigmoid(gate_wide)
    silu_val = gate_wide * logistic
    hidden = (silu_val * up_wide).astype(BF16)
    gate_slope = up_wide * logistic * (1.0 + gate_wide * (1.0 - logistic))

    far, act_rows, silu_val, gate_slope, hidden = lax.optimization_barrier(
        (far, act_rows, silu_val, gate_slope, hidden)
    )
    part, power = decode(coded)
    far_part, far_power = decode(far)
    coded = encode(part + far_part, jnp.minimum(power, far_power) - 1.0)
    coded = lax.all_gather(coded, QUAD, axis=0, tiled=False)
    coded_other = swap(coded, "c")

    grad_down_weight = dot(hidden, grad_rows, 1, 0)

    own, other = decode(coded)[0].reshape(800, 512), decode(coded_other)[0].reshape(800, 512)
    grad_hidden = by_core(own, other)
    grads = jnp.concatenate([grad_hidden * gate_slope, grad_hidden * silu_val]).astype(BF16)
    share = dot(grads, jnp.concatenate([gate_weight, up_weight], axis=1), 0, 1).astype(BF16)
    share = with_layout_constraint(share, Layout(major_to_minor=(0, 1)))
    share = lax.all_to_all(share.reshape(16, 64, 320), PLANE, 0, 0, tiled=True)
    share = jnp.sum(share.astype(F32), axis=0)
    grad_input = share[:32] + swap(share[32:], "h")

    grad_gate_weight = dot(act_rows, grads[:800], 0, 1)
    grad_up_weight = dot(act_rows, grads[800:], 0, 1)
    return (grad_input, grad_gate_weight, grad_up_weight, grad_down_weight)


def solution(mesh):
    fine = Mesh(mesh.devices.reshape(tuple(SIZES.values())), tuple(SIZES))
    wide, units, down = P(COL, ROW), P(ROW, COL), P(COL, ROW)
    return jax.shard_map(
        shards,
        mesh=fine,
        in_specs=(wide, wide, units, units, units, units, down),
        out_specs=(wide, units, units, down),
        check_vma=False,
    )
```
